512 devices in a mesh: occ: 64 (over x, z_lo, y), slab: 8 (over z_hi, core).
Axes of the slice: x: 4, y: 4, z: 16 (z_hi: 4, z_lo: 4; z = z_hi * 4 + z_lo), core: 2. Of those that a mesh axis runs over, the one named last changes fastest.
Arguments:
- amplitudes: bfloat16 [65536, 6144], P('occ', 'slab'), may hold values from -6 to 6
- integrals: bfloat16 [1024, 6144], P('occ', 'slab'), may hold values from -0.078125 to 0.078125
- prior_amplitudes: bfloat16 [1024, 65536], P('slab', 'occ'), may hold values from -1.796875 to 1.796875
- occ_counts: int32 [64], replicated, may hold values from 1 to 4, 160 in all
- occ_energy: float32 [160], replicated, may hold values from -2 to -0.5
- pair_orbitals: int32 [2, 512], replicated, may hold values from 0 to 999
- virt_energy: float32 [1000], replicated, may hold values from 0.1 to 4
Outputs:
- new_amps: float32 [1024, 65536], P('slab', 'occ')
The draws below stay inside these ranges and needn't reach their ends.
Inputs may be any that keep to these rules, and one draw needn't show every extreme that they name: occ_counts sums to 160; some block holds exactly 4.
All inputs are finite; a program needn't handle non-finite values.
Results may differ from the reference program's by a relative error of at most 0.0003.
Values may be sent and summed in bfloat16 or wider, within the bound.
A program may use at most 64 MiB of HBM per device.

```python
import math
import jax
import jax.numpy as jnp
import numpy as np
from jax import lax

NV = 1000
CAPI = 4
GROUP = 128
OCC_SLOT_TOTAL = 256
NOCC = 160
PAIRS = 65536
VIRTUAL_PAIR_ROWS = 1024
CD = 6144
N_OCC = 64


def with_ends(entries, own_key, smallest, high):
    place = [jax.random.randint(jax.random.fold_in(own_key, axis), (), 0, length) for axis, length in enumerate(entries.shape)]
    longest = entries.shape.index(max(entries.shape))
    neighbour = place[:longest] + [(place[longest] + 1) % entries.shape[longest]] + place[longest + 1:]
    return entries.at[tuple(place)].set(smallest).at[tuple(neighbour)].set(high)


def steps_of(own_key, dims, pieces, least, high):
    def one(dim, blocks):
        heights = jax.random.uniform(jax.random.fold_in(jax.random.fold_in(own_key, 6), dim), (blocks,), jnp.float32, least / len(pieces), high / len(pieces))
        return jnp.repeat(jnp.exp(heights), dims[dim] // blocks).reshape((-1,) + (1,) * (len(dims) - dim - 1))

    gain = one(*pieces[0])
    for cut in pieces[1:]:
        gain = gain * one(*cut)
    return gain


def split_up(amount, total, reach, lean):
    loads = [(1 << 20) // math.isqrt(grade ** lean) + 1 for grade in range(2, amount + 1)]
    surplus, given = total - reach - (amount - 1), [1] * (amount - 1)
    while surplus > 0:
        movable = [i for i in range(amount - 1) if given[i] < reach]
        mass, budget = sum([loads[i] for i in movable]), surplus
        for i in movable:
            extra = min(reach - given[i], max(1, budget * loads[i] // mass), surplus)
            given[i] = given[i] + extra
            surplus = surplus - extra
    return np.array([reach] + given)


def ragged_sizes(stream_key, number_of, total, limit, slope):
    if number_of == 2:
        one = jax.random.randint(stream_key, (), max(1, total - limit), min(limit, total - 1) + 1)
        return jnp.stack([one, total - one])
    sizes = jnp.asarray(split_up(number_of, total, limit, slope), jnp.int32)
    couples = (number_of - 1) // 2
    giver, receiver = sizes[1:1 + 2 * couples:2], sizes[2:2 + 2 * couples:2]
    margin = jnp.minimum(giver - 1, limit - receiver)
    shifted = jax.random.randint(jax.random.fold_in(stream_key, 1), (couples,), 0, 1 << 20) % (margin + 1)
    sizes = sizes.at[1:1 + 2 * couples:2].set(giver - shifted).at[2:2 + 2 * couples:2].set(receiver + shifted)
    return sizes[jax.random.permutation(jax.random.fold_in(stream_key, 2), number_of)]


def gaussian(rng, extent, spread, limit, pieces=(), held_as=jnp.bfloat16):
    array = jax.random.normal(rng, extent, jnp.float32) * spread
    if len(pieces) > 0:
        array = steps_of(rng, extent, pieces, -0.22, 0.18) * array
    return jnp.clip(array, min=-limit, max=limit).astype(held_as)


def setup_inputs(seed: int = 0) -> dict:
    key_list = jax.random.split(jax.random.key(seed), 8)
    amplitudes = gaussian(key_list[0], (PAIRS, CD), 1.0, 6.0, ((0, 64), (1, 8)))
    integrals = gaussian(key_list[1], (VIRTUAL_PAIR_ROWS, CD), CD ** -0.5, 0.078125, ((0, 64), (1, 8)))
    prior_amplitudes = gaussian(key_list[2], (VIRTUAL_PAIR_ROWS, PAIRS), 0.3, 1.796875, ((0, 8), (1, 64)))
    occ_counts = ragged_sizes(key_list[3], N_OCC, NOCC, CAPI, 2).astype(jnp.int32)
    occ_energy = jnp.clip(jax.random.uniform(key_list[4], (NOCC,), jnp.float32, -2.0, -0.5), -2.0, -0.5)
    pair_orbitals = with_ends(jax.random.randint(key_list[5], (2, VIRTUAL_PAIR_ROWS // 2), 0, NV), jax.random.fold_in(key_list[5], 1), 0, NV - 1).astype(jnp.int32)
    virt_energy = jnp.clip(jnp.exp(jax.random.uniform(key_list[6], (NV,), jnp.float32, math.log(0.1), math.log(4.0))), 0.1, 4.0)
    return dict(amplitudes=amplitudes, integrals=integrals, prior_amplitudes=prior_amplitudes, occ_counts=occ_counts, occ_energy=occ_energy, pair_orbitals=pair_orbitals, virt_energy=virt_energy)


def slot_tables(occ_counts, occ_energy):
    offsets = jnp.cumsum(occ_counts) - occ_counts
    within = jnp.arange(CAPI, dtype=jnp.int32)
    orbital = (offsets[:, None] + within[None, :]).reshape(-1).astype(jnp.int32)
    live = (within[None, :] < occ_counts[:, None]).reshape(-1)
    match = orbital[:, None] == jnp.arange(NOCC, dtype=jnp.int32)[None, :]
    energy = jnp.sum(jnp.where(match, occ_energy[None, :], 0.0), axis=1)
    return jnp.where(live, energy, 0.0), live


def column_energy(pair_orbitals, virt_energy):
    labels = jnp.arange(NV, dtype=jnp.int32)[None, :]
    first = jnp.sum(jnp.where(pair_orbitals[0][:, None] == labels, virt_energy[None, :], 0.0), axis=1)
    second = jnp.sum(jnp.where(pair_orbitals[1][:, None] == labels, virt_energy[None, :], 0.0), axis=1)
    half_sum = (first + second).reshape(VIRTUAL_PAIR_ROWS // GROUP, 1, GROUP // 2)
    return jnp.broadcast_to(half_sum, (VIRTUAL_PAIR_ROWS // GROUP, 2, GROUP // 2)).reshape(VIRTUAL_PAIR_ROWS)


def mirror_columns(values):
    shape = values.shape
    grouped = values.reshape((shape[0] // GROUP, 2, GROUP // 2) + shape[1:])
    return grouped[:, ::-1].reshape(shape)


def reference(amplitudes, integrals, prior_amplitudes, occ_counts, occ_energy, pair_orbitals, virt_energy):
    slot_energy, live = slot_tables(occ_counts, occ_energy)
    pair_energy = column_energy(pair_orbitals, virt_energy)
    ladder_contraction = lax.dot_general(integrals, amplitudes, (((1,), (1,)), ((), ())), preferred_element_type=jnp.float32)
    ladder_contraction = ladder_contraction.reshape(VIRTUAL_PAIR_ROWS, OCC_SLOT_TOTAL, OCC_SLOT_TOTAL)
    paired_contraction = ladder_contraction + jnp.transpose(mirror_columns(ladder_contraction), (0, 2, 1))
    energy_denominator = slot_energy[None, :, None] + slot_energy[None, None, :] - pair_energy[:, None, None]
    both_live = (live[:, None] & live[None, :])[None]
    refreshed_amplitudes = prior_amplitudes.reshape(VIRTUAL_PAIR_ROWS, OCC_SLOT_TOTAL, OCC_SLOT_TOTAL).astype(jnp.float32) + paired_contraction / energy_denominator
    return jnp.where(both_live, refreshed_amplitudes, 0.0).reshape(VIRTUAL_PAIR_ROWS, PAIRS)
```

```python
import functools

import jax
import jax.numpy as jnp
from jax import lax
from jax.experimental import pallas as pl
from jax.experimental.pallas import tpu as pltpu
from jax.sharding import PartitionSpec as P

CAPI = 4
GROUP = 128
NOCC = 160
SLOTS = 256
LIVE = CAPI * NOCC
MESH = pl.DeviceIdType.MESH
F32 = jnp.float32
BF16 = jnp.bfloat16


def halves(values):
    high = values.astype(BF16)
    return high, (values - high.astype(F32)).astype(BF16)


def dot_nt(left, right):
    return lax.dot_general(left, right, (((1,), (1,)), ((), ())), preferred_element_type=F32)


def dot_nn(left, right):
    return jnp.dot(left, right, preferred_element_type=F32)


def kernel(
    orb_ref, energy_ref, pair_ref, v_hbm, a_hbm, prior_hbm, out_ref,
    vb, amps, prior, packed, onehot, part, core_in, summed, ladder,
    up_out, down_out, up_in, down_in, up2_out, down2_out, up2_in, down2_in,
    turned, arrived,
    local_sem, z_send, z_recv, x_send, x_recv, y_send, y_recv, f_send, f_recv,
    c_send, c_recv, r_send, r_recv, e_send, e_recv,
):
    o = lax.axis_index("occ")
    s = lax.axis_index("slab")
    x, zl, y = o // 16, (o // 4) % 4, o % 4
    h, core = s // 2, s % 2
    other = 1 - core

    def at(value):
        return lax.rem(value + 8, 4)

    def place(px, pzl, py):
        return px * 16 + pzl * 4 + py

    def remote(src, dst, send, recv, occ, slab):
        return pltpu.make_async_remote_copy(
            src_ref=src, dst_ref=dst, send_sem=send, recv_sem=recv,
            device_id=(occ, slab), device_id_type=MESH,
        )

    sends = []

    def start(src, dst, send, recv, occ, slab):
        copy = remote(src, dst, send, recv, occ, slab)
        copy.start()
        sends.append(copy)

    def landed(dst, send, recv):
        remote(dst, dst, send, recv, lax.rem(o + 1, 64), s).wait_recv()

    get_v = pltpu.make_async_copy(v_hbm, vb.at[y, x, zl], local_sem.at[0])
    get_a = pltpu.make_async_copy(a_hbm, amps, local_sem.at[1])
    get_prior = pltpu.make_async_copy(prior_hbm, prior, local_sem.at[2])
    get_v.start()
    get_a.start()
    get_prior.start()

    barrier = pltpu.get_barrier_semaphore()

    def greet(t, carry):
        pl.semaphore_signal(
            barrier, inc=1, device_id=(lax.rem(o + t, 64), s), device_id_type=MESH
        )
        return carry

    lax.fori_loop(1, 64, greet, 0)
    up, down = 2 * at(h + 1) + core, 2 * at(h - 1) + core
    sibling = 2 * h + other
    for slab in (up, down, sibling):
        pl.semaphore_signal(barrier, inc=1, device_id=(o, slab), device_id_type=MESH)
    get_v.wait()
    pl.semaphore_wait(barrier, 66)

    for d in (1, 2, 3):
        start(vb.at[y, x, zl], vb.at[y, x, zl], z_send.at[d], z_recv.at[d], place(x, at(zl + d), y), s)

    match = lax.broadcasted_iota(jnp.int32, (NOCC, SLOTS), 0) == orb_ref[...]
    pick = jnp.where(match, 1.0, 0.0).astype(BF16)
    get_a.wait()
    for i in range(CAPI):
        packed[i * NOCC:(i + 1) * NOCC, :] = dot_nn(
            pick, amps[i * SLOTS:(i + 1) * SLOTS, :]
        ).astype(BF16)

    for d in (1, 2, 3):
        landed(vb.at[y, x, at(zl - d)], z_send.at[d], z_recv.at[d])

    x_next, x_back = place(at(x + 1), zl, y), place(at(x - 1), zl, y)
    y_next, y_back = place(x, zl, at(y + 1)), place(x, zl, at(y - 1))
    offsets = (0, -1, 1, 2)

    def y_piece(n):
        ref = vb.at[y, at(x + offsets[n])]
        start(ref, ref, y_send.at[n], y_recv.at[n], y_next, s)
        start(ref, ref, y_send.at[4 + n], y_recv.at[4 + n], y_back, s)

    def y_forward(n):
        px = at(x + offsets[n])
        landed(vb.at[at(y - 1), px], y_send.at[n], y_recv.at[n])
        ref = vb.at[at(y - 1), px, pl.ds(0, 2)]
        start(ref, ref, f_send.at[n], f_recv.at[n], y_next, s)
        landed(vb.at[at(y + 1), px], y_send.at[4 + n], y_recv.at[4 + n])
        ref = vb.at[at(y + 1), px, pl.ds(2, 2)]
        start(ref, ref, f_send.at[4 + n], f_recv.at[4 + n], y_back, s)

    ref = vb.at[y, x]
    start(ref, ref, x_send.at[0], x_recv.at[0], x_next, s)
    start(ref, ref, x_send.at[1], x_recv.at[1], x_back, s)
    y_piece(0)
    landed(vb.at[y, at(x - 1)], x_send.at[0], x_recv.at[0])
    ref = vb.at[y, at(x - 1), pl.ds(0, 2)]
    start(ref, ref, x_send.at[2], x_recv.at[2], x_next, s)
    landed(vb.at[y, at(x + 1)], x_send.at[1], x_recv.at[1])
    ref = vb.at[y, at(x + 1), pl.ds(2, 2)]
    start(ref, ref, x_send.at[3], x_recv.at[3], x_back, s)
    y_piece(1)
    y_piece(2)
    landed(vb.at[y, at(x + 2), pl.ds(0, 2)], x_send.at[2], x_recv.at[2])
    landed(vb.at[y, at(x + 2), pl.ds(2, 2)], x_send.at[3], x_recv.at[3])
    y_piece(3)

    steps = (0, 1, -1, 2)

    def multiply(t):
        block = vb[at(y + steps[t])].reshape(256, vb.shape[-1])
        part[t] = dot_nt(block, packed[...]).reshape(4, 2, 32, LIVE)
        start(part.at[t, :, other], core_in.at[t], c_send.at[t], c_recv.at[t], o, sibling)

    def add_cores(t):
        landed(core_in.at[t], c_send.at[t], c_recv.at[t])
        summed[t] = part[t, :, core] + core_in[t]
        up_out[t, 0] = summed[t, at(h + 1), 0:16]
        up_out[t, 1] = summed[t, at(h + 2), 16:32]
        down_out[t, 0] = summed[t, at(h - 2), 0:16]
        down_out[t, 1] = summed[t, at(h - 1), 16:32]
        start(up_out.at[t], up_in.at[t], r_send.at[t], r_recv.at[t], o, up)
        start(down_out.at[t], down_in.at[t], r_send.at[4 + t], r_recv.at[4 + t], o, down)

    def second(t):
        landed(up_in.at[t], r_send.at[t], r_recv.at[t])
        up2_out[t] = summed[t, at(h + 1), 16:32] + up_in[t, 1]
        start(up2_out.at[t], up2_in.at[t], r_send.at[8 + t], r_recv.at[8 + t], o, up)
        landed(down_in.at[t], r_send.at[4 + t], r_recv.at[4 + t])
        down2_out[t] = summed[t, at(h - 1), 0:16] + down_in[t, 0]
        start(down2_out.at[t], down2_in.at[t], r_send.at[12 + t], r_recv.at[12 + t], o, down)

    def finish(t):
        landed(up2_in.at[t], r_send.at[8 + t], r_recv.at[8 + t])
        landed(down2_in.at[t], r_send.at[12 + t], r_recv.at[12 + t])
        row = at(y + steps[t])
        ladder[0, row] = summed[t, h, 0:16] + up_in[t, 0] + down2_in[t]
        ladder[1, row] = summed[t, h, 16:32] + down_in[t, 1] + up2_in[t]

    multiply(0)
    y_forward(0)
    add_cores(0)
    y_forward(1)
    y_forward(2)
    y_forward(3)
    multiply(1)
    multiply(2)
    second(0)
    add_cores(1)
    add_cores(2)

    row_id = lax.broadcasted_iota(jnp.int32, (1024, SLOTS), 0)
    lane_id = lax.broadcasted_iota(jnp.int32, (1024, SLOTS), 1)
    orbital = jnp.sum(
        jnp.where(lane_id == (row_id >> 2), orb_ref[...].astype(F32), 0.0), axis=1, keepdims=True
    ).astype(jnp.int32)
    slot_i = lax.broadcasted_iota(jnp.int32, (1024, 1), 0) & 3
    column = jnp.where(orbital >= 0, slot_i * NOCC + orbital, -1)
    onehot[...] = jnp.where(
        lax.broadcasted_iota(jnp.int32, (1024, LIVE), 1) == column, 1.0, 0.0
    ).astype(BF16)

    for n in range(4):
        px = at(x + offsets[n])
        landed(vb.at[at(y + 2), px, pl.ds(0, 2)], f_send.at[n], f_recv.at[n])
        landed(vb.at[at(y + 2), px, pl.ds(2, 2)], f_send.at[4 + n], f_recv.at[4 + n])
    multiply(3)
    second(1)
    second(2)
    add_cores(3)
    finish(0)
    finish(1)
    finish(2)
    second(3)
    finish(3)

    low = ladder[0].reshape(GROUP // 2, LIVE)
    top = ladder[1].reshape(GROUP // 2, LIVE)
    high, rest = halves(jnp.concatenate([top, low], axis=0))
    turned[...] = dot_nt(onehot[...], high) + dot_nt(onehot[...], rest)

    def rows(b):
        return pl.ds(pl.multiple_of(b * 16, 16), 16)

    def exchange(t, b):
        return remote(
            turned.at[rows(b)], arrived.at[rows(o)], e_send.at[t], e_recv.at[t], b, s
        )

    def send(t, carry):
        exchange(t, lax.rem(o + t, 64)).start()
        return carry

    lax.fori_loop(1, 64, send, 0)
    arrived[rows(o), :] = turned[rows(o), :]

    high, rest = halves(jnp.concatenate([low, top], axis=0))
    own = []
    for q in range(CAPI):
        cut = slice(q * NOCC, (q + 1) * NOCC)
        own.append(dot_nn(high[:, cut], pick) + dot_nn(rest[:, cut], pick))
    get_prior.wait()

    spread = jnp.where(
        lax.broadcasted_iota(jnp.int32, (SLOTS, SLOTS), 1)
        == ((lax.broadcasted_iota(jnp.int32, (SLOTS, SLOTS), 0) & 63) * 4
            + (lax.broadcasted_iota(jnp.int32, (SLOTS, SLOTS), 0) >> 6)),
        1.0, 0.0,
    ).astype(BF16)

    for copy in sends:
        copy.wait_send()

    def receive(t, carry):
        b = lax.rem(o + 64 - t, 64)
        remote(arrived.at[rows(b)], arrived.at[rows(b)], e_send.at[t], e_recv.at[t], b, s).wait_recv()
        exchange(t, lax.rem(o + t, 64)).wait_send()
        return carry

    lax.fori_loop(1, 64, receive, 0)

    slot_id = lax.broadcasted_iota(jnp.int32, (1, SLOTS), 1)
    live = jnp.where(orb_ref[...] >= 0, 1.0, 0.0)
    for q in range(CAPI):
        block = jnp.concatenate(
            [arrived[pl.ds(q * CAPI + i, 64, stride=16), :] for i in range(CAPI)], axis=0
        )
        high, rest = halves(jnp.transpose(block))
        paired = own[q] + (dot_nn(high, spread) + dot_nn(rest, spread))
        mine = slot_id == o * CAPI + q
        energy = jnp.sum(jnp.where(mine, energy_ref[...], 0.0), axis=1, keepdims=True)
        alive = jnp.sum(jnp.where(mine, live, 0.0), axis=1, keepdims=True)
        cut = slice(q * SLOTS, (q + 1) * SLOTS)
        fresh = prior[:, cut].astype(F32) + paired / ((energy + energy_ref[...]) - pair_ref[...])
        out_ref[:, cut] = jnp.where(alive * live > 0.5, fresh, 0.0)


def per_device(
    amplitudes, integrals, prior_amplitudes, occ_counts, occ_energy, pair_orbitals, virt_energy
):
    depth = amplitudes.shape[1]
    offsets = jnp.cumsum(occ_counts) - occ_counts
    within = jnp.arange(CAPI, dtype=jnp.int32)
    live = (within[None, :] < occ_counts[:, None]).reshape(-1)
    orbital = jnp.where(live, (offsets[:, None] + within[None, :]).reshape(-1), -1)
    match = orbital[:, None] == jnp.arange(NOCC, dtype=jnp.int32)[None, :]
    slot_energy = jnp.sum(jnp.where(match, occ_energy[None, :], 0.0), axis=1)
    labels = jnp.arange(virt_energy.shape[0], dtype=jnp.int32)[None, :]
    mine = lax.dynamic_slice_in_dim(
        pair_orbitals, lax.axis_index("slab") * (GROUP // 2), GROUP // 2, 1
    )
    virtual = jnp.sum(
        jnp.where(mine[:, :, None] == labels[None], virt_energy[None, None, :], 0.0), axis=2
    )
    half_sum = virtual[0] + virtual[1]
    pair_energy = jnp.concatenate([half_sum, half_sum])[:, None]
    any_spec = pl.BlockSpec(memory_space=pl.ANY)
    vmem_spec = pl.BlockSpec(memory_space=pltpu.VMEM)
    dma = pltpu.SemaphoreType.DMA
    return pl.pallas_call(
        kernel,
        out_shape=jax.ShapeDtypeStruct((GROUP, CAPI * SLOTS), F32),
        in_specs=[vmem_spec] * 3 + [any_spec] * 3,
        out_specs=vmem_spec,
        scratch_shapes=[
            pltpu.VMEM((4, 4, 4, 16, depth), BF16),
            pltpu.VMEM((CAPI * SLOTS, depth), BF16),
            pltpu.VMEM((GROUP, CAPI * SLOTS), BF16),
            pltpu.VMEM((LIVE, depth), BF16),
            pltpu.VMEM((1024, LIVE), BF16),
            pltpu.VMEM((4, 4, 2, 32, LIVE), F32),
            pltpu.VMEM((4, 4, 32, LIVE), F32),
            pltpu.VMEM((4, 4, 32, LIVE), F32),
            pltpu.VMEM((2, 4, 16, LIVE), F32),
        ]
        + [pltpu.VMEM((4, 2, 16, LIVE), F32)] * 4
        + [pltpu.VMEM((4, 16, LIVE), F32)] * 4
        + [pltpu.VMEM((1024, GROUP), F32)] * 2
        + [
            dma((3,)), dma((4,)), dma((4,)), dma((4,)), dma((4,)), dma((8,)), dma((8,)), dma((8,)), dma((8,)),
            dma((4,)), dma((4,)), dma((16,)), dma((16,)), dma((64,)), dma((64,)),
        ],
        compiler_params=pltpu.CompilerParams(
            collective_id=0, has_side_effects=True, vmem_limit_bytes=44 * 1024 * 1024
        ),
        cost_estimate=pl.CostEstimate(flops=2 * 1024 * 640 * 768, bytes_accessed=3 << 20, transcendentals=0),
    )(orbital[None, :], slot_energy[None, :], pair_energy, integrals, amplitudes, prior_amplitudes)


def solution(mesh):
    return jax.shard_map(
        per_device,
        mesh=mesh,
        in_specs=(P("occ", "slab"), P("occ", "slab"), P("slab", "occ"), P(), P(), P(), P()),
        out_specs=P("slab", "occ"),
        check_vma=False,
    )
```

```python
import functools

import jax
import jax.numpy as jnp
from jax import lax
from jax.experimental import pallas as pl
from jax.experimental.pallas import tpu as pltpu
from jax.sharding import PartitionSpec as P

CAPI = 4
GROUP = 128
NOCC = 160
SLOTS = 256
LIVE = CAPI * NOCC
MESH = pl.DeviceIdType.MESH
F32 = jnp.float32
BF16 = jnp.bfloat16


def halves(values):
    high = values.astype(BF16)
    return high, (values - high.astype(F32)).astype(BF16)


def dot_nt(left, right):
    return lax.dot_general(left, right, (((1,), (1,)), ((), ())), preferred_element_type=F32)


def dot_nn(left, right):
    return jnp.dot(left, right, preferred_element_type=F32)


def kernel(
    v_hbm, a_hbm, prior_hbm, counts_hbm, occ_hbm, pairs_hbm, virt_hbm, out_ref,
    vb, amps, prior, counts, occ_energy, pairs, virt, packed, onehot, part, core_in, summed, ladder,
    up_out, down_out, up_in, down_in, up2_out, down2_out, up2_in, down2_in,
    up_top, down_top, up_top_in, down_top_in, up2_top, down2_top, up2_top_in, down2_top_in,
    turned, arrived,
    local_sem, z_send, z_recv, x_send, x_recv, y_send, y_recv, f_send, f_recv,
    c_send, c_recv, r_send, r_recv, m_send, m_recv, e_send, e_recv,
):
    o = lax.axis_index("occ")
    s = lax.axis_index("slab")
    x, zl, y = o // 16, (o // 4) % 4, o % 4
    h, core = s // 2, s % 2
    other = 1 - core

    def at(value):
        return lax.rem(value + 8, 4)

    def place(px, pzl, py):
        return px * 16 + pzl * 4 + py

    def remote(src, dst, send, recv, occ, slab):
        return pltpu.make_async_remote_copy(
            src_ref=src, dst_ref=dst, send_sem=send, recv_sem=recv,
            device_id=(occ, slab), device_id_type=MESH,
        )

    sends = []

    def start(src, dst, send, recv, occ, slab):
        copy = remote(src, dst, send, recv, occ, slab)
        copy.start()
        sends.append(copy)

    def landed(dst, send, recv):
        remote(dst, dst, send, recv, lax.rem(o + 1, 64), s).wait_recv()

    get_v = pltpu.make_async_copy(v_hbm, vb.at[y, x, zl], local_sem.at[0])
    get_a = pltpu.make_async_copy(a_hbm, amps, local_sem.at[1])
    get_prior = pltpu.make_async_copy(prior_hbm, prior, local_sem.at[2])
    small = [
        pltpu.make_async_copy(src, dst, local_sem.at[3 + n])
        for n, (src, dst) in enumerate(
            ((counts_hbm, counts), (occ_hbm, occ_energy), (pairs_hbm, pairs), (virt_hbm, virt))
        )
    ]
    get_v.start()
    for copy in small:
        copy.start()
    get_a.start()
    get_prior.start()

    barrier = pltpu.get_barrier_semaphore()

    up, down = 2 * at(h + 1) + core, 2 * at(h - 1) + core
    sibling = 2 * h + other
    x_next, x_back = place(at(x + 1), zl, y), place(at(x - 1), zl, y)
    y_next, y_back = place(x, zl, at(y + 1)), place(x, zl, at(y - 1))
    partners = [(place(x, at(zl + d), y), s) for d in (1, 2, 3)]
    partners += [(x_next, s), (x_back, s), (y_next, s), (y_back, s)]
    partners += [(o, up), (o, down), (o, sibling)]
    for partner in partners:
        pl.semaphore_signal(barrier, inc=1, device_id=partner, device_id_type=MESH)
    get_v.wait()
    pl.semaphore_wait(barrier, len(partners))

    for d in (1, 2, 3):
        start(vb.at[y, x, zl], vb.at[y, x, zl], z_send.at[d], z_recv.at[d], place(x, at(zl + d), y), s)

    for copy in small:
        copy.wait()
    slot_id = lax.broadcasted_iota(jnp.int32, (1, SLOTS), 1)
    block_id = lax.broadcasted_iota(jnp.int32, (64, SLOTS), 0)
    block_of = lax.broadcasted_iota(jnp.int32, (64, SLOTS), 1) >> 2
    held = jnp.broadcast_to(counts[...].astype(F32), (8, 64)).astype(BF16)
    before = dot_nn(held, jnp.where(block_id < block_of, 1.0, 0.0).astype(BF16))[0:1]
    own_count = dot_nn(held, jnp.where(block_id == block_of, 1.0, 0.0).astype(BF16))[0:1]
    within = (slot_id & 3).astype(F32)
    orbital_row = jnp.where(within < own_count, before + within, -1.0)
    match = lax.broadcasted_iota(jnp.int32, (NOCC, SLOTS), 0).astype(F32) == orbital_row
    pick = jnp.where(match, 1.0, 0.0).astype(BF16)
    get_a.wait()
    for i in range(CAPI):
        packed[i * NOCC:(i + 1) * NOCC, :] = dot_nn(
            pick, amps[i * SLOTS:(i + 1) * SLOTS, :]
        ).astype(BF16)

    rest = jnp.broadcast_to(occ_energy[...], (8, NOCC))
    energy_row = jnp.zeros((8, SLOTS), F32)
    for _ in range(3):
        piece = rest.astype(BF16)
        rest = rest - piece.astype(F32)
        energy_row = energy_row + dot_nn(piece, pick)
    energy_row = energy_row[0:1]
    pair_total = pairs.shape[1]
    wanted = s * (GROUP // 2) + (lax.broadcasted_iota(jnp.int32, (GROUP, pair_total), 0) & 63)
    chosen = lax.broadcasted_iota(jnp.int32, (GROUP, pair_total), 1) == wanted
    label = lax.broadcasted_iota(jnp.int32, (GROUP, virt.shape[1]), 1).astype(F32)
    pair_energy = jnp.zeros((GROUP, 1), F32)
    for n in range(2):
        orbital = jnp.sum(
            jnp.where(chosen, pairs[n:n + 1, :].astype(F32), 0.0), axis=1, keepdims=True
        )
        pair_energy = pair_energy + jnp.sum(
            jnp.where(label == orbital, virt[...], 0.0), axis=1, keepdims=True
        )

    for d in (1, 2, 3):
        landed(vb.at[y, x, at(zl - d)], z_send.at[d], z_recv.at[d])

    offsets = (0, -1, 1, 2)

    def y_piece(n):
        ref = vb.at[y, at(x + offsets[n])]
        start(ref, ref, y_send.at[n], y_recv.at[n], y_next, s)
        start(ref, ref, y_send.at[4 + n], y_recv.at[4 + n], y_back, s)

    def y_forward(n):
        px = at(x + offsets[n])
        landed(vb.at[at(y - 1), px], y_send.at[n], y_recv.at[n])
        ref = vb.at[at(y - 1), px, pl.ds(0, 2)]
        start(ref, ref, f_send.at[n], f_recv.at[n], y_next, s)
        landed(vb.at[at(y + 1), px], y_send.at[4 + n], y_recv.at[4 + n])
        ref = vb.at[at(y + 1), px, pl.ds(2, 2)]
        start(ref, ref, f_send.at[4 + n], f_recv.at[4 + n], y_back, s)

    ref = vb.at[y, x]
    start(ref, ref, x_send.at[0], x_recv.at[0], x_next, s)
    start(ref, ref, x_send.at[1], x_recv.at[1], x_back, s)
    y_piece(0)
    landed(vb.at[y, at(x - 1)], x_send.at[0], x_recv.at[0])
    ref = vb.at[y, at(x - 1), pl.ds(0, 2)]
    start(ref, ref, x_send.at[2], x_recv.at[2], x_next, s)
    landed(vb.at[y, at(x + 1)], x_send.at[1], x_recv.at[1])
    ref = vb.at[y, at(x + 1), pl.ds(2, 2)]
    start(ref, ref, x_send.at[3], x_recv.at[3], x_back, s)
    y_piece(1)
    y_piece(2)
    landed(vb.at[y, at(x + 2), pl.ds(0, 2)], x_send.at[2], x_recv.at[2])
    landed(vb.at[y, at(x + 2), pl.ds(2, 2)], x_send.at[3], x_recv.at[3])
    y_piece(3)

    steps = (0, 1, -1, 2)

    def multiply(t):
        block = vb[at(y + steps[t])].reshape(256, vb.shape[-1])
        part[t] = dot_nt(block, packed[...]).reshape(4, 2, 32, LIVE)
        start(part.at[t, :, other], core_in.at[t], c_send.at[t], c_recv.at[t], o, sibling)

    eye = lax.broadcasted_iota(jnp.int32, (32, GROUP), 0) == lax.broadcasted_iota(
        jnp.int32, (32, GROUP), 1
    )

    def code(values, out, top_out):
        rows = values.shape[0]
        top = jnp.maximum(jnp.max(jnp.abs(values), axis=1, keepdims=True), 1e-30)
        coded = jnp.round(values * (32767.0 / top)).astype(jnp.int32).astype(jnp.int16)
        out[...] = coded.reshape(out.shape)
        top_out[...] = jnp.sum(jnp.where(eye[:rows], top, 0.0), axis=0, keepdims=True)

    def decode(coded, top_row):
        rows = coded.shape[0]
        top = jnp.sum(jnp.where(eye[:rows], top_row, 0.0), axis=1, keepdims=True)
        return coded.astype(F32) * (top * (1.0 / 32767.0))

    def send_coded(n, values, out, top_out, into, top_into, slab):
        code(values, out, top_out)
        start(out, into, r_send.at[n], r_recv.at[n], o, slab)
        start(top_out, top_into, m_send.at[n], m_recv.at[n], o, slab)

    def landed_coded(n, into, top_into):
        landed(into, r_send.at[n], r_recv.at[n])
        landed(top_into, m_send.at[n], m_recv.at[n])
        return decode(into[...].reshape(-1, LIVE), top_into[...])

    def add_cores(t):
        landed(core_in.at[t], c_send.at[t], c_recv.at[t])
        summed[t] = part[t, :, core] + core_in[t]
        up_values = jnp.concatenate([summed[t, at(h + 1), 0:16], summed[t, at(h + 2), 16:32]])
        send_coded(t, up_values, up_out.at[t], up_top.at[t], up_in.at[t], up_top_in.at[t], up)
        down_values = jnp.concatenate([summed[t, at(h - 2), 0:16], summed[t, at(h - 1), 16:32]])
        send_coded(
            4 + t, down_values, down_out.at[t], down_top.at[t], down_in.at[t], down_top_in.at[t], down
        )

    def second(t):
        values = landed_coded(t, up_in.at[t], up_top_in.at[t])
        summed[t, h, 0:16] = summed[t, h, 0:16] + values[0:16]
        send_coded(
            8 + t, summed[t, at(h + 1), 16:32] + values[16:32],
            up2_out.at[t], up2_top.at[t], up2_in.at[t], up2_top_in.at[t], up,
        )
        values = landed_coded(4 + t, down_in.at[t], down_top_in.at[t])
        summed[t, h, 16:32] = summed[t, h, 16:32] + values[16:32]
        send_coded(
            12 + t, summed[t, at(h - 1), 0:16] + values[0:16],
            down2_out.at[t], down2_top.at[t], down2_in.at[t], down2_top_in.at[t], down,
        )

    def finish(t):
        row = at(y + steps[t])
        ladder[0, row] = summed[t, h, 0:16] + landed_coded(12 + t, down2_in.at[t], down2_top_in.at[t])
        ladder[1, row] = summed[t, h, 16:32] + landed_coded(8 + t, up2_in.at[t], up2_top_in.at[t])

    multiply(0)
    y_forward(0)
    add_cores(0)
    y_forward(1)
    y_forward(2)
    y_forward(3)
    multiply(1)
    multiply(2)
    second(0)
    add_cores(1)
    add_cores(2)

    row_id = lax.broadcasted_iota(jnp.int32, (1024, SLOTS), 0)
    lane_id = lax.broadcasted_iota(jnp.int32, (1024, SLOTS), 1)
    orbital = jnp.sum(
        jnp.where(lane_id == (row_id >> 2), orbital_row, 0.0), axis=1, keepdims=True
    ).astype(jnp.int32)
    slot_i = lax.broadcasted_iota(jnp.int32, (1024, 1), 0) & 3
    column = jnp.where(orbital >= 0, slot_i * NOCC + orbital, -1)
    onehot[...] = jnp.where(
        lax.broadcasted_iota(jnp.int32, (1024, LIVE), 1) == column, 1.0, 0.0
    ).astype(BF16)

    for n in range(4):
        px = at(x + offsets[n])
        landed(vb.at[at(y + 2), px, pl.ds(0, 2)], f_send.at[n], f_recv.at[n])
        landed(vb.at[at(y + 2), px, pl.ds(2, 2)], f_send.at[4 + n], f_recv.at[4 + n])
    multiply(3)
    second(1)
    second(2)
    add_cores(3)
    finish(0)
    finish(1)
    finish(2)
    second(3)
    finish(3)

    low = ladder[0].reshape(GROUP // 2, LIVE)
    top = ladder[1].reshape(GROUP // 2, LIVE)
    high, rest = halves(jnp.concatenate([top, low], axis=0))
    turned[...] = dot_nt(onehot[...], high) + dot_nt(onehot[...], rest)

    def rows(b):
        return pl.ds(pl.multiple_of(b * 16, 16), 16)

    def exchange(t, b):
        return remote(
            turned.at[rows(b)], arrived.at[rows(o)], e_send.at[t], e_recv.at[t], b, s
        )

    def send(t, carry):
        exchange(t, lax.rem(o + t, 64)).start()
        return carry

    lax.fori_loop(1, 64, send, 0)
    arrived[rows(o), :] = turned[rows(o), :]

    high, rest = halves(jnp.concatenate([low, top], axis=0))
    own = []
    for q in range(CAPI):
        cut = slice(q * NOCC, (q + 1) * NOCC)
        own.append(dot_nn(high[:, cut], pick) + dot_nn(rest[:, cut], pick))
    get_prior.wait()

    spread = jnp.where(
        lax.broadcasted_iota(jnp.int32, (SLOTS, SLOTS), 1)
        == ((lax.broadcasted_iota(jnp.int32, (SLOTS, SLOTS), 0) & 63) * 4
            + (lax.broadcasted_iota(jnp.int32, (SLOTS, SLOTS), 0) >> 6)),
        1.0, 0.0,
    ).astype(BF16)

    for copy in sends:
        copy.wait_send()

    def receive(t, carry):
        b = lax.rem(o + 64 - t, 64)
        remote(arrived.at[rows(b)], arrived.at[rows(b)], e_send.at[t], e_recv.at[t], b, s).wait_recv()
        exchange(t, lax.rem(o + t, 64)).wait_send()
        return carry

    lax.fori_loop(1, 64, receive, 0)

    live = jnp.where(orbital_row >= 0.0, 1.0, 0.0)
    for q in range(CAPI):
        block = jnp.concatenate(
            [arrived[pl.ds(q * CAPI + i, 64, stride=16), :] for i in range(CAPI)], axis=0
        )
        high, rest = halves(jnp.transpose(block))
        paired = own[q] + (dot_nn(high, spread) + dot_nn(rest, spread))
        mine = slot_id == o * CAPI + q
        energy = jnp.sum(jnp.where(mine, energy_row, 0.0), axis=1, keepdims=True)
        alive = jnp.sum(jnp.where(mine, live, 0.0), axis=1, keepdims=True)
        cut = slice(q * SLOTS, (q + 1) * SLOTS)
        fresh = prior[:, cut].astype(F32) + paired / ((energy + energy_row) - pair_energy)
        out_ref[:, cut] = jnp.where(alive * live > 0.5, fresh, 0.0)


def per_device(
    amplitudes, integrals, prior_amplitudes, occ_counts, occ_energy, pair_orbitals, virt_energy
):
    depth = amplitudes.shape[1]
    pair_count, virt_count = pair_orbitals.shape[1], virt_energy.shape[0]
    any_spec = pl.BlockSpec(memory_space=pl.ANY)
    vmem_spec = pl.BlockSpec(memory_space=pltpu.VMEM)
    dma = pltpu.SemaphoreType.DMA
    return pl.pallas_call(
        kernel,
        out_shape=jax.ShapeDtypeStruct((GROUP, CAPI * SLOTS), F32),
        in_specs=[any_spec] * 7,
        out_specs=vmem_spec,
        scratch_shapes=[
            pltpu.VMEM((4, 4, 4, 16, depth), BF16),
            pltpu.VMEM((CAPI * SLOTS, depth), BF16),
            pltpu.VMEM((GROUP, CAPI * SLOTS), BF16),
            pltpu.VMEM((1, occ_counts.shape[0]), jnp.int32),
            pltpu.VMEM((1, NOCC), F32),
            pltpu.VMEM((2, pair_count), jnp.int32),
            pltpu.VMEM((1, virt_count), F32),
            pltpu.VMEM((LIVE, depth), BF16),
            pltpu.VMEM((1024, LIVE), BF16),
            pltpu.VMEM((4, 4, 2, 32, LIVE), F32),
            pltpu.VMEM((4, 4, 32, LIVE), F32),
            pltpu.VMEM((4, 4, 32, LIVE), F32),
            pltpu.VMEM((2, 4, 16, LIVE), F32),
        ]
        + [pltpu.VMEM((4, 2, 16, LIVE), jnp.int16)] * 4
        + [pltpu.VMEM((4, 16, LIVE), jnp.int16)] * 4
        + [pltpu.VMEM((4, 1, GROUP), F32)] * 8
        + [pltpu.VMEM((1024, GROUP), F32)] * 2
        + [
            dma((7,)), dma((4,)), dma((4,)), dma((4,)), dma((4,)), dma((8,)), dma((8,)), dma((8,)), dma((8,)),
            dma((4,)), dma((4,)), dma((16,)), dma((16,)), dma((16,)), dma((16,)), dma((64,)), dma((64,)),
        ],
        compiler_params=pltpu.CompilerParams(
            collective_id=0, has_side_effects=True, vmem_limit_bytes=60 * 1024 * 1024
        ),
        cost_estimate=pl.CostEstimate(flops=2 * 1024 * 640 * 768, bytes_accessed=3 << 20, transcendentals=0),
    )(
        integrals, amplitudes, prior_amplitudes,
        occ_counts[None, :], occ_energy[None, :], pair_orbitals, virt_energy[None, :],
    )


def solution(mesh):
    return jax.shard_map(
        per_device,
        mesh=mesh,
        in_specs=(P("occ", "slab"), P("occ", "slab"), P("slab", "occ"), P(), P(), P(), P()),
        out_specs=P("slab", "occ"),
        check_vma=False,
    )
```

```python
import functools

import jax
import jax.numpy as jnp
from jax import lax
from jax.experimental import pallas as pl
from jax.experimental.pallas import tpu as pltpu
from jax.sharding import PartitionSpec as P

CAPI = 4
GROUP = 128
NOCC = 160
SLOTS = 256
LIVE = CAPI * NOCC
MESH = pl.DeviceIdType.MESH
F32 = jnp.float32
BF16 = jnp.bfloat16


def halves(values):
    high = values.astype(BF16)
    return high, (values - high.astype(F32)).astype(BF16)


def dot_nt(left, right):
    return lax.dot_general(left, right, (((1,), (1,)), ((), ())), preferred_element_type=F32)


def dot_nn(left, right):
    return jnp.dot(left, right, preferred_element_type=F32)


def kernel(
    v_hbm, a_hbm, prior_hbm, counts_hbm, occ_hbm, pairs_hbm, virt_hbm, out_ref,
    vb, amps, prior, counts, occ_energy, pairs, virt, packed, onehot, part, core_in, summed, ladder,
    r_out, r_in, top_out, top_in,
    turned, arrived, peaks, opened,
    local_sem, z_send, z_recv, y_send, y_recv, f_send, f_recv,
    c_send, c_recv, r_send, r_recv, m_send, m_recv, e_send, e_recv, p_send, p_recv,
):
    o = lax.axis_index("occ")
    s = lax.axis_index("slab")
    x, zl, y = o // 16, (o // 4) % 4, o % 4
    h, core = s // 2, s % 2
    other = 1 - core

    def at(value):
        return lax.rem(value + 8, 4)

    def place(px, pzl, py):
        return px * 16 + pzl * 4 + py

    def remote(src, dst, send, recv, occ, slab):
        return pltpu.make_async_remote_copy(
            src_ref=src, dst_ref=dst, send_sem=send, recv_sem=recv,
            device_id=(occ, slab), device_id_type=MESH,
        )

    sends = []

    def start(src, dst, send, recv, occ, slab):
        copy = remote(src, dst, send, recv, occ, slab)
        copy.start()
        sends.append(copy)

    def landed(dst, send, recv):
        remote(dst, dst, send, recv, lax.rem(o + 1, 64), s).wait_recv()

    barrier = pltpu.get_barrier_semaphore()
    up, down = 2 * at(h + 1) + core, 2 * at(h - 1) + core
    sibling = 2 * h + other
    y_next, y_back = place(x, zl, at(y + 1)), place(x, zl, at(y - 1))
    partners = [(place(x, at(zl + d), y), s) for d in (1, 2, 3)]
    partners += [(place(at(x + d), zl, y), s) for d in (1, 2, 3)]
    partners += [(y_next, s), (y_back, s)]
    partners += [(o, up), (o, down), (o, sibling)]
    for partner in partners:
        pl.semaphore_signal(barrier, inc=1, device_id=partner, device_id_type=MESH)

    get_v = pltpu.make_async_copy(v_hbm, vb.at[y, zl % 2, x, zl // 2], local_sem.at[0])
    get_a = pltpu.make_async_copy(a_hbm, amps, local_sem.at[1])
    get_prior = pltpu.make_async_copy(prior_hbm, prior, local_sem.at[2])
    small = [
        pltpu.make_async_copy(src, dst, local_sem.at[3 + n])
        for n, (src, dst) in enumerate(
            ((counts_hbm, counts), (occ_hbm, occ_energy), (pairs_hbm, pairs), (virt_hbm, virt))
        )
    ]
    get_v.start()
    for copy in small:
        copy.start()
    get_a.start()
    get_prior.start()

    get_v.wait()
    pl.semaphore_wait(barrier, len(partners))

    def block_at(px, pzl):
        return vb.at[y, pzl % 2, px, pzl // 2]

    for d in (2, 1, 3):
        start(
            block_at(x, zl), block_at(x, zl), z_send.at[d], z_recv.at[d], place(x, at(zl + d), y), s
        )
    for d in (2, 1, 3):
        landed(block_at(x, at(zl - d)), z_send.at[d], z_recv.at[d])
    for k in (0, 1):
        for dx in (2, 1, 3):
            n = 4 + 4 * k + dx
            start(
                vb.at[y, k, x], vb.at[y, k, x], z_send.at[n], z_recv.at[n], place(at(x + dx), zl, y), s
            )

    for copy in small:
        copy.wait()
    slot_id = lax.broadcasted_iota(jnp.int32, (1, SLOTS), 1)
    block_id = lax.broadcasted_iota(jnp.int32, (64, SLOTS), 0)
    block_of = lax.broadcasted_iota(jnp.int32, (64, SLOTS), 1) >> 2
    held = jnp.broadcast_to(counts[...].astype(F32), (8, 64)).astype(BF16)
    before = dot_nn(held, jnp.where(block_id < block_of, 1.0, 0.0).astype(BF16))[0:1]
    own_count = dot_nn(held, jnp.where(block_id == block_of, 1.0, 0.0).astype(BF16))[0:1]
    within = (slot_id & 3).astype(F32)
    orbital_row = jnp.where(within < own_count, before + within, -1.0)
    match = lax.broadcasted_iota(jnp.int32, (NOCC, SLOTS), 0).astype(F32) == orbital_row
    pick = jnp.where(match, 1.0, 0.0).astype(BF16)
    get_a.wait()
    for i in range(CAPI):
        packed[i * NOCC:(i + 1) * NOCC, :] = dot_nn(
            pick, amps[i * SLOTS:(i + 1) * SLOTS, :]
        ).astype(BF16)

    def own_row(k):
        for dx in (2, 1, 3):
            n = 4 + 4 * k + dx
            landed(vb.at[y, k, at(x - dx)], z_send.at[n], z_recv.at[n])
        ref = vb.at[y, k]
        start(ref, ref, y_send.at[k], y_recv.at[k], y_next, s)
        start(ref, ref, y_send.at[2 + k], y_recv.at[2 + k], y_back, s)

    def forward(k):
        landed(vb.at[at(y - 1), k], y_send.at[k], y_recv.at[k])
        ref = vb.at[at(y - 1), k, pl.ds(0, 2)]
        start(ref, ref, f_send.at[k], f_recv.at[k], y_next, s)
        landed(vb.at[at(y + 1), k], y_send.at[2 + k], y_recv.at[2 + k])
        ref = vb.at[at(y + 1), k, pl.ds(2, 2)]
        start(ref, ref, f_send.at[2 + k], f_recv.at[2 + k], y_back, s)

    def far_row(k):
        landed(vb.at[at(y + 2), k, pl.ds(0, 2)], f_send.at[k], f_recv.at[k])
        landed(vb.at[at(y + 2), k, pl.ds(2, 2)], f_send.at[2 + k], f_recv.at[2 + k])

    parts = ((0, 0), (0, 1), (1, 0), (-1, 0), (1, 1), (-1, 1), (2, 0), (2, 1))

    def multiply(*ts):
        blocks = []
        for t in ts:
            step, k = parts[t]
            blocks.append(vb[at(y + step), k].reshape(128, vb.shape[-1]))
        product = dot_nt(jnp.concatenate(blocks, axis=0), packed[...])
        for n, t in enumerate(ts):
            part[t] = product[128 * n:128 * (n + 1)].reshape(4, 2, 16, LIVE)
            start(part.at[t, :, other], core_in.at[t], c_send.at[t], c_recv.at[t], o, sibling)

    eye = lax.broadcasted_iota(jnp.int32, (16, GROUP), 0) == lax.broadcasted_iota(
        jnp.int32, (16, GROUP), 1
    )

    def code(values, out, top_out):
        top = jnp.maximum(jnp.max(jnp.abs(values), axis=1, keepdims=True), 1e-30)
        out[...] = jnp.round(values * (32767.0 / top)).astype(jnp.int32).astype(jnp.int16)
        top_out[...] = jnp.sum(jnp.where(eye, top, 0.0), axis=0, keepdims=True)

    def decode(coded, top_row):
        top = jnp.sum(jnp.where(eye, top_row, 0.0), axis=1, keepdims=True)
        return coded.astype(F32) * (top * (1.0 / 32767.0))

    def ahead(t):
        return (up, 1) if t % 2 else (down, -1)

    def behind(t):
        return ahead(t + 1)

    def send_coded(n, values, slab):
        code(values, r_out.at[n], top_out.at[n])
        start(r_out.at[n], r_in.at[n], r_send.at[n], r_recv.at[n], o, slab)
        start(top_out.at[n], top_in.at[n], m_send.at[n], m_recv.at[n], o, slab)

    def landed_coded(n):
        landed(r_in.at[n], r_send.at[n], r_recv.at[n])
        landed(top_in.at[n], m_send.at[n], m_recv.at[n])
        return decode(r_in[n], top_in[n])

    def add_cores(t):
        landed(core_in.at[t], c_send.at[t], c_recv.at[t])
        summed[t] = part[t, :, core] + core_in[t]
        send_coded(3 * t, summed[t, at(h + 2)], ahead(t)[0])
        slab, step = behind(t)
        send_coded(3 * t + 1, summed[t, at(h + step)], slab)

    def second(t):
        slab, step = ahead(t)
        values = summed[t, at(h + step)] + landed_coded(3 * t)
        send_coded(3 * t + 2, values, slab)

    def finish(t):
        step, k = parts[t]
        ladder[k, at(y + step)] = (
            summed[t, h] + landed_coded(3 * t + 1) + landed_coded(3 * t + 2)
        )

    own_row(0)
    multiply(0)
    own_row(1)
    multiply(1)
    add_cores(0)
    add_cores(1)

    rest = jnp.broadcast_to(occ_energy[...], (8, NOCC))
    energy_row = jnp.zeros((8, SLOTS), F32)
    for _ in range(3):
        piece = rest.astype(BF16)
        rest = rest - piece.astype(F32)
        energy_row = energy_row + dot_nn(piece, pick)
    energy_row = energy_row[0:1]
    pair_total = pairs.shape[1]
    wanted = s * (GROUP // 2) + (lax.broadcasted_iota(jnp.int32, (GROUP, pair_total), 0) & 63)
    chosen = lax.broadcasted_iota(jnp.int32, (GROUP, pair_total), 1) == wanted
    label = lax.broadcasted_iota(jnp.int32, (GROUP, virt.shape[1]), 1).astype(F32)
    pair_energy = jnp.zeros((GROUP, 1), F32)
    for n in range(2):
        orbital = jnp.sum(
            jnp.where(chosen, pairs[n:n + 1, :].astype(F32), 0.0), axis=1, keepdims=True
        )
        pair_energy = pair_energy + jnp.sum(
            jnp.where(label == orbital, virt[...], 0.0), axis=1, keepdims=True
        )

    row_id = lax.broadcasted_iota(jnp.int32, (1024, SLOTS), 0)
    lane_id = lax.broadcasted_iota(jnp.int32, (1024, SLOTS), 1)
    orbital = jnp.sum(
        jnp.where(lane_id == (row_id >> 2), orbital_row, 0.0), axis=1, keepdims=True
    ).astype(jnp.int32)
    slot_i = lax.broadcasted_iota(jnp.int32, (1024, 1), 0) & 3
    column = jnp.where(orbital >= 0, slot_i * NOCC + orbital, -1)
    onehot[...] = jnp.where(
        lax.broadcasted_iota(jnp.int32, (1024, LIVE), 1) == column, 1.0, 0.0
    ).astype(BF16)

    forward(0)
    multiply(2, 3)
    add_cores(2)
    add_cores(3)
    forward(1)
    multiply(4, 5)
    add_cores(4)
    add_cores(5)
    far_row(0)
    multiply(6)
    add_cores(6)
    far_row(1)
    multiply(7)
    add_cores(7)
    for t in range(8):
        second(t)
    for t in range(8):
        finish(t)

    low = ladder[0].reshape(GROUP // 2, LIVE)
    top = ladder[1].reshape(GROUP // 2, LIVE)
    mirrored = jnp.concatenate([top, low], axis=0)
    peak = jnp.maximum(jnp.max(jnp.abs(mirrored), axis=1, keepdims=True), 1e-30)
    diagonal = lax.broadcasted_iota(jnp.int32, (GROUP, GROUP), 0) == lax.broadcasted_iota(
        jnp.int32, (GROUP, GROUP), 1
    )
    peaks[o] = jnp.sum(jnp.where(diagonal, peak, 0.0), axis=0, keepdims=True)

    def rows(b):
        return pl.ds(pl.multiple_of(b * 16, 16), 16)

    def exchange_peak(t, b):
        return remote(peaks.at[o], peaks.at[o], p_send.at[t], p_recv.at[t], b, s)

    def exchange(t, b):
        return remote(
            turned.at[rows(b)], arrived.at[rows(o)], e_send.at[t], e_recv.at[t], b, s
        )

    def send_peak(t, carry):
        exchange_peak(t, lax.rem(o + t, 64)).start()
        return carry

    def send(t, carry):
        exchange(t, lax.rem(o + t, 64)).start()
        return carry

    lax.fori_loop(1, 64, send_peak, 0)
    whole = jnp.round(mirrored * (32767.0 / peak))
    coarse = jnp.round(whole * (1.0 / 256.0))
    fine = (whole - 256.0 * coarse).astype(BF16)
    turned[...] = (
        256.0 * dot_nt(onehot[...], coarse.astype(BF16)) + dot_nt(onehot[...], fine)
    ).astype(jnp.int32).astype(jnp.int16)
    lax.fori_loop(1, 64, send, 0)
    arrived[rows(o), :] = turned[rows(o), :]

    high, rest = halves(jnp.concatenate([low, top], axis=0))
    own = []
    for q in range(CAPI):
        cut = slice(q * NOCC, (q + 1) * NOCC)
        own.append(dot_nn(high[:, cut], pick) + dot_nn(rest[:, cut], pick))
    get_prior.wait()

    spread = jnp.where(
        lax.broadcasted_iota(jnp.int32, (SLOTS, SLOTS), 1)
        == ((lax.broadcasted_iota(jnp.int32, (SLOTS, SLOTS), 0) & 63) * 4
            + (lax.broadcasted_iota(jnp.int32, (SLOTS, SLOTS), 0) >> 6)),
        1.0, 0.0,
    ).astype(BF16)

    for copy in sends:
        copy.wait_send()

    def receive(t, carry):
        b = lax.rem(o + 64 - t, 64)
        remote(arrived.at[rows(b)], arrived.at[rows(b)], e_send.at[t], e_recv.at[t], b, s).wait_recv()
        remote(peaks.at[b], peaks.at[b], p_send.at[t], p_recv.at[t], b, s).wait_recv()
        exchange(t, lax.rem(o + t, 64)).wait_send()
        exchange_peak(t, lax.rem(o + t, 64)).wait_send()
        return carry

    lax.fori_loop(1, 64, receive, 0)

    opened[...] = (
        arrived[...].astype(F32).reshape(64, 16, GROUP) * (peaks[...] * (1.0 / 32767.0))
    ).reshape(1024, GROUP)
    live = jnp.where(orbital_row >= 0.0, 1.0, 0.0)
    for q in range(CAPI):
        block = jnp.concatenate(
            [opened[pl.ds(q * CAPI + i, 64, stride=16), :] for i in range(CAPI)], axis=0
        )
        high, rest = halves(jnp.transpose(block))
        paired = own[q] + (dot_nn(high, spread) + dot_nn(rest, spread))
        mine = slot_id == o * CAPI + q
        energy = jnp.sum(jnp.where(mine, energy_row, 0.0), axis=1, keepdims=True)
        alive = jnp.sum(jnp.where(mine, live, 0.0), axis=1, keepdims=True)
        cut = slice(q * SLOTS, (q + 1) * SLOTS)
        fresh = prior[:, cut].astype(F32) + paired / ((energy + energy_row) - pair_energy)
        out_ref[:, cut] = jnp.where(alive * live > 0.5, fresh, 0.0)


def per_device(
    amplitudes, integrals, prior_amplitudes, occ_counts, occ_energy, pair_orbitals, virt_energy
):
    depth = amplitudes.shape[1]
    pair_count, virt_count = pair_orbitals.shape[1], virt_energy.shape[0]
    hbm_spec = pl.BlockSpec(memory_space=pltpu.HBM)
    vmem_spec = pl.BlockSpec(memory_space=pltpu.VMEM)
    dma = pltpu.SemaphoreType.DMA
    return pl.pallas_call(
        kernel,
        out_shape=pltpu.VMEM((GROUP, CAPI * SLOTS), F32),
        in_specs=[hbm_spec] * 7,
        out_specs=vmem_spec,
        scratch_shapes=[
            pltpu.VMEM((4, 2, 4, 2, 16, depth), BF16),
            pltpu.VMEM((CAPI * SLOTS, depth), BF16),
            pltpu.VMEM((GROUP, CAPI * SLOTS), BF16),
            pltpu.VMEM((1, occ_counts.shape[0]), jnp.int32),
            pltpu.VMEM((1, NOCC), F32),
            pltpu.VMEM((2, pair_count), jnp.int32),
            pltpu.VMEM((1, virt_count), F32),
            pltpu.VMEM((LIVE, depth), BF16),
            pltpu.VMEM((1024, LIVE), BF16),
            pltpu.VMEM((8, 4, 2, 16, LIVE), F32),
            pltpu.VMEM((8, 4, 16, LIVE), F32),
            pltpu.VMEM((8, 4, 16, LIVE), F32),
            pltpu.VMEM((2, 4, 16, LIVE), F32),
        ]
        + [pltpu.VMEM((24, 16, LIVE), jnp.int16)] * 2
        + [pltpu.VMEM((24, 1, GROUP), F32)] * 2
        + [pltpu.VMEM((1024, GROUP), jnp.int16)] * 2
        + [pltpu.VMEM((64, 1, GROUP), F32), pltpu.VMEM((1024, GROUP), F32)]
        + [
            dma((7,)), dma((16,)), dma((16,)), dma((8,)), dma((8,)), dma((8,)), dma((8,)),
            dma((8,)), dma((8,)), dma((24,)), dma((24,)), dma((24,)), dma((24,)), dma((64,)), dma((64,)),
            dma((64,)), dma((64,)),
        ],
        compiler_params=pltpu.CompilerParams(
            collective_id=0, has_side_effects=True, vmem_limit_bytes=58 * 1024 * 1024
        ),
        cost_estimate=pl.CostEstimate(flops=2 * 1024 * 640 * 768, bytes_accessed=3 << 20, transcendentals=0),
    )(
        integrals, amplitudes, prior_amplitudes,
        occ_counts[None, :], occ_energy[None, :], pair_orbitals, virt_energy[None, :],
    )


def solution(mesh):
    return jax.shard_map(
        per_device,
        mesh=mesh,
        in_specs=(P("occ", "slab"), P("occ", "slab"), P("slab", "occ"), P(), P(), P(), P()),
        out_specs=P("slab", "occ"),
        check_vma=False,
    )
```

```python
import functools

import jax
import jax.numpy as jnp
from jax import lax
from jax.experimental import pallas as pl
from jax.experimental.pallas import tpu as pltpu
from jax.sharding import PartitionSpec as P

CAPI = 4
GROUP = 128
NOCC = 160
SLOTS = 256
LIVE = CAPI * NOCC
MESH = pl.DeviceIdType.MESH
F32 = jnp.float32
BF16 = jnp.bfloat16


def halves(values):
    high = values.astype(BF16)
    return high, (values - high.astype(F32)).astype(BF16)


def dot_nt(left, right):
    return lax.dot_general(left, right, (((1,), (1,)), ((), ())), preferred_element_type=F32)


def dot_nn(left, right):
    return jnp.dot(left, right, preferred_element_type=F32)


def kernel(
    v_hbm, a_hbm, prior_hbm, counts_hbm, occ_hbm, pairs_hbm, virt_hbm, out_ref,
    vb, amps, prior, counts, occ_energy, pairs, virt, packed, onehot, part, core_in, summed, ladder,
    r_out, r_in, top_out, top_in,
    turned, arrived, peaks, opened,
    near_sem, far_sem,
    local_sem, z_send, z_recv, x_send, x_recv, y_send, y_recv, f_send, f_recv, s_send, s_recv,
    c_send, c_recv, r_send, r_recv, m_send, m_recv, e_send, e_recv, p_send, p_recv,
):
    o = lax.axis_index("occ")
    s = lax.axis_index("slab")
    x, zl, y = o // 16, (o // 4) % 4, o % 4
    h, core = s // 2, s % 2
    other = 1 - core

    def at(value):
        return lax.rem(value + 8, 4)

    def place(px, pzl, py):
        return px * 16 + pzl * 4 + py

    def remote(src, dst, send, recv, occ, slab):
        return pltpu.make_async_remote_copy(
            src_ref=src, dst_ref=dst, send_sem=send, recv_sem=recv,
            device_id=(occ, slab), device_id_type=MESH,
        )

    sends = []

    def start(src, dst, send, recv, occ, slab):
        copy = remote(src, dst, send, recv, occ, slab)
        copy.start()
        sends.append(copy)

    def landed(dst, send, recv):
        remote(dst, dst, send, recv, lax.rem(o + 1, 64), s).wait_recv()

    barrier = pltpu.get_barrier_semaphore()
    up, down = 2 * at(h + 1) + core, 2 * at(h - 1) + core
    sibling = 2 * h + other
    near = [place(x, at(zl + d), y) for d in (1, 2, 3)]
    near += [place(at(x + d), zl, y) for d in (1, 2, 3)]
    near += [place(x, zl, at(y + d)) for d in (1, 2, 3)]

    def greet(occ, slab):
        pl.semaphore_signal(barrier, inc=1, device_id=(occ, slab), device_id_type=MESH)

    greet(o, sibling)
    for occ in near:
        greet(occ, 2 * h)
    for step in (1, -1):
        greet(o, 2 * at(h + step) + 1)

    def tell(sem):
        pl.semaphore_signal(sem, inc=1, device_id=(o, sibling), device_id_type=MESH)

    def meet_near():
        @pl.when(core == 0)
        def _():
            pl.semaphore_wait(barrier, 2 * len(near) + 1)
            tell(near_sem)

        @pl.when(core == 1)
        def _():
            pl.semaphore_wait(near_sem, 1)

    def meet_far():
        @pl.when(core == 1)
        def _():
            pl.semaphore_wait(barrier, 5)
            tell(far_sem)

        @pl.when(core == 0)
        def _():
            pl.semaphore_wait(far_sem, 1)

    get_v = pltpu.make_async_copy(v_hbm, vb.at[y, zl % 2, x, zl // 2], local_sem.at[0])
    get_a = pltpu.make_async_copy(a_hbm, amps, local_sem.at[1])
    get_prior = pltpu.make_async_copy(prior_hbm, prior, local_sem.at[2])
    small = [
        pltpu.make_async_copy(src, dst, local_sem.at[3 + n])
        for n, (src, dst) in enumerate(
            ((counts_hbm, counts), (occ_hbm, occ_energy), (pairs_hbm, pairs), (virt_hbm, virt))
        )
    ]
    get_v.start()
    for copy in small:
        copy.start()
    get_a.start()
    get_prior.start()

    get_v.wait()
    meet_near()

    def block_at(px, pzl):
        return vb.at[y, pzl % 2, px, pzl // 2]

    for d in (2, 1, 3):
        start(
            block_at(x, zl), block_at(x, zl), z_send.at[d], z_recv.at[d], place(x, at(zl + d), y), s
        )
    for d in (2, 1, 3):
        landed(block_at(x, at(zl - d)), z_send.at[d], z_recv.at[d])

    for k in (0, 1):
        ref = vb.at[y, k, x]
        for d in (2, 1, 3):
            n = 4 * k + d
            start(ref, ref, x_send.at[n], x_recv.at[n], place(at(x + d), zl, y), s)
        for d in (1, 3, 2):
            n = 4 * k + d
            start(ref, ref, y_send.at[n], y_recv.at[n], place(x, zl, at(y + d)), s)

    for copy in small:
        copy.wait()
    slot_id = lax.broadcasted_iota(jnp.int32, (1, SLOTS), 1)
    block_id = lax.broadcasted_iota(jnp.int32, (64, SLOTS), 0)
    block_of = lax.broadcasted_iota(jnp.int32, (64, SLOTS), 1) >> 2
    held = jnp.broadcast_to(counts[...].astype(F32), (8, 64)).astype(BF16)
    before = dot_nn(held, jnp.where(block_id < block_of, 1.0, 0.0).astype(BF16))[0:1]
    own_count = dot_nn(held, jnp.where(block_id == block_of, 1.0, 0.0).astype(BF16))[0:1]
    within = (slot_id & 3).astype(F32)
    orbital_row = jnp.where(within < own_count, before + within, -1.0)
    match = lax.broadcasted_iota(jnp.int32, (NOCC, SLOTS), 0).astype(F32) == orbital_row
    pick = jnp.where(match, 1.0, 0.0).astype(BF16)
    get_a.wait()
    for i in range(CAPI):
        packed[i * NOCC:(i + 1) * NOCC, :] = dot_nn(
            pick, amps[i * SLOTS:(i + 1) * SLOTS, :]
        ).astype(BF16)

    def own_row(k):
        for d in (2, 1, 3):
            landed(vb.at[y, k, at(x - d)], x_send.at[4 * k + d], x_recv.at[4 * k + d])

    def opposite(k):
        ref = vb.at[y, k, at(x + 2)]
        for d in (1, 3, 2):
            n = 4 * k + d
            start(ref, ref, f_send.at[n], f_recv.at[n], place(x, zl, at(y + d)), s)

    def pass_on(k, d):
        n = 4 * k + d
        ref = vb.at[at(y - d), k, x]
        landed(ref, y_send.at[n], y_recv.at[n])
        start(ref, ref, s_send.at[2 * n], s_recv.at[2 * n], place(at(x + 1), zl, y), s)
        start(ref, ref, s_send.at[2 * n + 1], s_recv.at[2 * n + 1], place(at(x - 1), zl, y), s)

    def other_row(k, d):
        n = 4 * k + d
        row = at(y - d)
        landed(vb.at[row, k, at(x + 2)], f_send.at[n], f_recv.at[n])
        landed(vb.at[row, k, at(x - 1)], s_send.at[2 * n], s_recv.at[2 * n])
        landed(vb.at[row, k, at(x + 1)], s_send.at[2 * n + 1], s_recv.at[2 * n + 1])

    parts = ((0, 0), (0, 1), (1, 0), (-1, 0), (1, 1), (-1, 1), (2, 0), (2, 1))

    def multiply(*ts):
        blocks = []
        for t in ts:
            step, k = parts[t]
            blocks.append(vb[at(y + step), k].reshape(128, vb.shape[-1]))
        product = dot_nt(jnp.concatenate(blocks, axis=0), packed[...])
        for n, t in enumerate(ts):
            part[t] = product[128 * n:128 * (n + 1)].reshape(4, 2, 16, LIVE)
            start(part.at[t, :, other], core_in.at[t], c_send.at[t], c_recv.at[t], o, sibling)

    eye = lax.broadcasted_iota(jnp.int32, (16, GROUP), 0) == lax.broadcasted_iota(
        jnp.int32, (16, GROUP), 1
    )

    def code(values, out, top_out):
        top = jnp.maximum(jnp.max(jnp.abs(values), axis=1, keepdims=True), 1e-30)
        out[...] = jnp.round(values * (32767.0 / top)).astype(jnp.int32).astype(jnp.int16)
        top_out[...] = jnp.sum(jnp.where(eye, top, 0.0), axis=0, keepdims=True)

    def decode(coded, top_row):
        top = jnp.sum(jnp.where(eye, top_row, 0.0), axis=1, keepdims=True)
        return coded.astype(F32) * (top * (1.0 / 32767.0))

    def ahead(t):
        return (up, 1) if t % 2 else (down, -1)

    def behind(t):
        return ahead(t + 1)

    def send_coded(n, values, slab):
        code(values, r_out.at[n], top_out.at[n])
        start(r_out.at[n], r_in.at[n], r_send.at[n], r_recv.at[n], o, slab)
        start(top_out.at[n], top_in.at[n], m_send.at[n], m_recv.at[n], o, slab)

    def landed_coded(n):
        landed(r_in.at[n], r_send.at[n], r_recv.at[n])
        landed(top_in.at[n], m_send.at[n], m_recv.at[n])
        return decode(r_in[n], top_in[n])

    def add_cores(t):
        landed(core_in.at[t], c_send.at[t], c_recv.at[t])
        summed[t] = part[t, :, core] + core_in[t]
        send_coded(3 * t, summed[t, at(h + 2)], ahead(t)[0])
        slab, step = behind(t)
        send_coded(3 * t + 1, summed[t, at(h + step)], slab)

    def second(t):
        slab, step = ahead(t)
        values = summed[t, at(h + step)] + landed_coded(3 * t)
        send_coded(3 * t + 2, values, slab)

    def finish(t):
        step, k = parts[t]
        ladder[k, at(y + step)] = (
            summed[t, h] + landed_coded(3 * t + 1) + landed_coded(3 * t + 2)
        )

    pass_on(0, 1)
    pass_on(0, 3)
    own_row(0)
    multiply(0)
    opposite(0)
    pass_on(1, 1)
    pass_on(1, 3)
    own_row(1)
    multiply(1)
    opposite(1)
    pass_on(0, 2)
    meet_far()
    add_cores(0)
    pass_on(1, 2)
    add_cores(1)

    rest = jnp.broadcast_to(occ_energy[...], (8, NOCC))
    energy_row = jnp.zeros((8, SLOTS), F32)
    for _ in range(3):
        piece = rest.astype(BF16)
        rest = rest - piece.astype(F32)
        energy_row = energy_row + dot_nn(piece, pick)
    energy_row = energy_row[0:1]
    pair_total = pairs.shape[1]
    wanted = s * (GROUP // 2) + (lax.broadcasted_iota(jnp.int32, (GROUP, pair_total), 0) & 63)
    chosen = lax.broadcasted_iota(jnp.int32, (GROUP, pair_total), 1) == wanted
    label = lax.broadcasted_iota(jnp.int32, (GROUP, virt.shape[1]), 1).astype(F32)
    pair_energy = jnp.zeros((GROUP, 1), F32)
    for n in range(2):
        orbital = jnp.sum(
            jnp.where(chosen, pairs[n:n + 1, :].astype(F32), 0.0), axis=1, keepdims=True
        )
        pair_energy = pair_energy + jnp.sum(
            jnp.where(label == orbital, virt[...], 0.0), axis=1, keepdims=True
        )

    row_id = lax.broadcasted_iota(jnp.int32, (1024, SLOTS), 0)
    lane_id = lax.broadcasted_iota(jnp.int32, (1024, SLOTS), 1)
    wanted = (((row_id >> 6) & 3) << 6) + ((row_id >> 8) << 4) + ((row_id >> 2) & 15)
    orbital = jnp.sum(
        jnp.where(lane_id == wanted, orbital_row, 0.0), axis=1, keepdims=True
    ).astype(jnp.int32)
    slot_i = lax.broadcasted_iota(jnp.int32, (1024, 1), 0) & 3
    column = jnp.where(orbital >= 0, slot_i * NOCC + orbital, -1)
    onehot[...] = jnp.where(
        lax.broadcasted_iota(jnp.int32, (1024, LIVE), 1) == column, 1.0, 0.0
    ).astype(BF16)

    for t, k, d in ((2, 0, 3), (3, 0, 1), (4, 1, 3), (5, 1, 1), (6, 0, 2), (7, 1, 2)):
        other_row(k, d)
        multiply(t)
        if t >= 3:
            add_cores(t - 1)
    add_cores(7)
    for t in range(8):
        second(t)
    for t in range(8):
        finish(t)

    low = ladder[0].reshape(GROUP // 2, LIVE)
    top = ladder[1].reshape(GROUP // 2, LIVE)
    mirrored = jnp.concatenate([top, low], axis=0)
    peak = jnp.maximum(jnp.max(jnp.abs(mirrored), axis=1, keepdims=True), 1e-30)
    diagonal = lax.broadcasted_iota(jnp.int32, (GROUP, GROUP), 0) == lax.broadcasted_iota(
        jnp.int32, (GROUP, GROUP), 1
    )
    peaks[o] = jnp.sum(jnp.where(diagonal, peak, 0.0), axis=0, keepdims=True)

    def rows(b):
        return pl.ds(pl.multiple_of(b * 16, 16), 16)

    def exchange(dx, d, dy, sign=1):
        n = dx * 16 + d * 4 + dy
        px, pzl, py = at(x + sign * dx), at(zl + sign * d), at(y + sign * dy)
        b = place(px, pzl, py)
        source = o if sign > 0 else b
        return (
            remote(
                turned.at[rows(pzl * 16 + px * 4 + py)], arrived.at[rows(source)],
                e_send.at[n], e_recv.at[n], b, s,
            ),
            remote(peaks.at[source], peaks.at[source], p_send.at[n], p_recv.at[n], b, s),
        )

    whole = jnp.round(mirrored * (32767.0 / peak))
    coarse = jnp.round(whole * (1.0 / 256.0))
    fine = (whole - 256.0 * coarse).astype(BF16)
    coarse = coarse.astype(BF16)
    order = []
    for d in (2, 1, 3, 0):
        group = pl.ds(pl.multiple_of(at(zl + d) * 256, 256), 256)
        turned[group, :] = (
            256.0 * dot_nt(onehot[group, :], coarse) + dot_nt(onehot[group, :], fine)
        ).astype(jnp.int32).astype(jnp.int16)
        for dx in (2, 1, 3, 0):
            for dy in (2, 1, 3, 0):
                if dx or d or dy:
                    order.append((dx, d, dy))
                    for copy in exchange(dx, d, dy):
                        copy.start()
    arrived[rows(o), :] = turned[rows(zl * 16 + x * 4 + y), :]

    high, rest = halves(jnp.concatenate([low, top], axis=0))
    own = []
    for q in range(CAPI):
        cut = slice(q * NOCC, (q + 1) * NOCC)
        own.append(dot_nn(high[:, cut], pick) + dot_nn(rest[:, cut], pick))
    get_prior.wait()

    spread = jnp.where(
        lax.broadcasted_iota(jnp.int32, (SLOTS, SLOTS), 1)
        == ((lax.broadcasted_iota(jnp.int32, (SLOTS, SLOTS), 0) & 63) * 4
            + (lax.broadcasted_iota(jnp.int32, (SLOTS, SLOTS), 0) >> 6)),
        1.0, 0.0,
    ).astype(BF16)

    for copy in sends:
        copy.wait_send()

    for step in order:
        for copy in exchange(*step, sign=-1):
            copy.wait_recv()
        for copy in exchange(*step):
            copy.wait_send()

    opened[...] = (
        arrived[...].astype(F32).reshape(64, 16, GROUP) * (peaks[...] * (1.0 / 32767.0))
    ).reshape(1024, GROUP)
    live = jnp.where(orbital_row >= 0.0, 1.0, 0.0)
    for q in range(CAPI):
        block = jnp.concatenate(
            [opened[pl.ds(q * CAPI + i, 64, stride=16), :] for i in range(CAPI)], axis=0
        )
        high, rest = halves(jnp.transpose(block))
        paired = own[q] + (dot_nn(high, spread) + dot_nn(rest, spread))
        mine = slot_id == o * CAPI + q
        energy = jnp.sum(jnp.where(mine, energy_row, 0.0), axis=1, keepdims=True)
        alive = jnp.sum(jnp.where(mine, live, 0.0), axis=1, keepdims=True)
        cut = slice(q * SLOTS, (q + 1) * SLOTS)
        fresh = prior[:, cut].astype(F32) + paired / ((energy + energy_row) - pair_energy)
        out_ref[:, cut] = jnp.where(alive * live > 0.5, fresh, 0.0)


def per_device(
    amplitudes, integrals, prior_amplitudes, occ_counts, occ_energy, pair_orbitals, virt_energy
):
    depth = amplitudes.shape[1]
    pair_count, virt_count = pair_orbitals.shape[1], virt_energy.shape[0]
    hbm_spec = pl.BlockSpec(memory_space=pltpu.HBM)
    vmem_spec = pl.BlockSpec(memory_space=pltpu.VMEM)
    dma = pltpu.SemaphoreType.DMA
    return pl.pallas_call(
        kernel,
        out_shape=pltpu.VMEM((GROUP, CAPI * SLOTS), F32),
        in_specs=[hbm_spec] * 7,
        out_specs=vmem_spec,
        scratch_shapes=[
            pltpu.VMEM((4, 2, 4, 2, 16, depth), BF16),
            pltpu.VMEM((CAPI * SLOTS, depth), BF16),
            pltpu.VMEM((GROUP, CAPI * SLOTS), BF16),
            pltpu.VMEM((1, occ_counts.shape[0]), jnp.int32),
            pltpu.VMEM((1, NOCC), F32),
            pltpu.VMEM((2, pair_count), jnp.int32),
            pltpu.VMEM((1, virt_count), F32),
            pltpu.VMEM((LIVE, depth), BF16),
            pltpu.VMEM((1024, LIVE), BF16),
            pltpu.VMEM((8, 4, 2, 16, LIVE), F32),
            pltpu.VMEM((8, 4, 16, LIVE), F32),
            pltpu.VMEM((8, 4, 16, LIVE), F32),
            pltpu.VMEM((2, 4, 16, LIVE), F32),
        ]
        + [pltpu.VMEM((24, 16, LIVE), jnp.int16)] * 2
        + [pltpu.VMEM((24, 1, GROUP), F32)] * 2
        + [pltpu.VMEM((1024, GROUP), jnp.int16)] * 2
        + [pltpu.VMEM((64, 1, GROUP), F32), pltpu.VMEM((1024, GROUP), F32)]
        + [pltpu.SemaphoreType.REGULAR] * 2
        + [
            dma((7,)), dma((4,)), dma((4,)), dma((8,)), dma((8,)), dma((8,)), dma((8,)), dma((8,)), dma((8,)),
            dma((16,)), dma((16,)),
            dma((8,)), dma((8,)), dma((24,)), dma((24,)), dma((24,)), dma((24,)), dma((64,)), dma((64,)),
            dma((64,)), dma((64,)),
        ],
        compiler_params=pltpu.CompilerParams(
            collective_id=0, has_side_effects=True, vmem_limit_bytes=58 * 1024 * 1024
        ),
        cost_estimate=pl.CostEstimate(flops=2 * 1024 * 640 * 768, bytes_accessed=3 << 20, transcendentals=0),
    )(
        integrals, amplitudes, prior_amplitudes,
        occ_counts[None, :], occ_energy[None, :], pair_orbitals, virt_energy[None, :],
    )


def solution(mesh):
    return jax.shard_map(
        per_device,
        mesh=mesh,
        in_specs=(P("occ", "slab"), P("occ", "slab"), P("slab", "occ"), P(), P(), P(), P()),
        out_specs=P("slab", "occ"),
        check_vma=False,
    )
```

```python
import functools

import jax
import jax.numpy as jnp
from jax import lax
from jax.experimental import pallas as pl
from jax.experimental.pallas import tpu as pltpu
from jax.sharding import PartitionSpec as P

CAPI = 4
GROUP = 128
NOCC = 160
SLOTS = 256
LIVE = CAPI * NOCC
MESH = pl.DeviceIdType.MESH
F32 = jnp.float32
BF16 = jnp.bfloat16


def halves(values):
    high = values.astype(BF16)
    return high, (values - high.astype(F32)).astype(BF16)


def dot_nt(left, right):
    return lax.dot_general(left, right, (((1,), (1,)), ((), ())), preferred_element_type=F32)


def dot_nn(left, right):
    return jnp.dot(left, right, preferred_element_type=F32)


def kernel(
    v_hbm, a_hbm, prior_hbm, counts_hbm, occ_hbm, pairs_hbm, virt_hbm, out_ref,
    vb, amps, prior, counts, occ_energy, pairs, virt, packed, onehot, part, core_in, summed, ladder,
    r_out, r_in, top_out, top_in,
    turned, arrived, peaks, opened,
    near_sem, far_sem,
    local_sem, z_send, z_recv, x_send, x_recv, y_send, y_recv, f_send, f_recv, s_send, s_recv,
    c_send, c_recv, r_send, r_recv, m_send, m_recv, e_send, e_recv, p_send, p_recv,
):
    o = lax.axis_index("occ")
    s = lax.axis_index("slab")
    x, zl, y = o // 16, (o // 4) % 4, o % 4
    h, core = s // 2, s % 2
    other = 1 - core

    def at(value):
        return lax.rem(value + 8, 4)

    def place(px, pzl, py):
        return px * 16 + pzl * 4 + py

    def remote(src, dst, send, recv, occ, slab):
        return pltpu.make_async_remote_copy(
            src_ref=src, dst_ref=dst, send_sem=send, recv_sem=recv,
            device_id=(occ, slab), device_id_type=MESH,
        )

    sends = []

    def start(src, dst, send, recv, occ, slab):
        copy = remote(src, dst, send, recv, occ, slab)
        copy.start()
        sends.append(copy)

    def landed(dst, send, recv):
        remote(dst, dst, send, recv, lax.rem(o + 1, 64), s).wait_recv()

    barrier = pltpu.get_barrier_semaphore()
    up, down = 2 * at(h + 1) + core, 2 * at(h - 1) + core
    sibling = 2 * h + other
    near = [place(x, at(zl + d), y) for d in (1, 2, 3)]
    near += [place(at(x + d), zl, y) for d in (1, 2, 3)]
    near += [place(x, zl, at(y + d)) for d in (1, 2, 3)]

    def greet(occ, slab):
        pl.semaphore_signal(barrier, inc=1, device_id=(occ, slab), device_id_type=MESH)

    greet(o, sibling)
    for occ in near:
        greet(occ, 2 * h)
    for step in (1, -1):
        greet(o, 2 * at(h + step) + 1)

    def tell(sem):
        pl.semaphore_signal(sem, inc=1, device_id=(o, sibling), device_id_type=MESH)

    def meet_near():
        @pl.when(core == 0)
        def _():
            pl.semaphore_wait(barrier, 2 * len(near) + 1)
            tell(near_sem)

        @pl.when(core == 1)
        def _():
            pl.semaphore_wait(near_sem, 1)

    def meet_far():
        @pl.when(core == 1)
        def _():
            pl.semaphore_wait(barrier, 5)
            tell(far_sem)

        @pl.when(core == 0)
        def _():
            pl.semaphore_wait(far_sem, 1)

    get_v = pltpu.make_async_copy(v_hbm, vb.at[y, zl % 2, x, zl // 2], local_sem.at[0])
    get_a = pltpu.make_async_copy(a_hbm, amps, local_sem.at[1])
    get_prior = pltpu.make_async_copy(prior_hbm, prior, local_sem.at[2])
    small = [
        pltpu.make_async_copy(src, dst, local_sem.at[3 + n])
        for n, (src, dst) in enumerate(
            ((counts_hbm, counts), (occ_hbm, occ_energy), (pairs_hbm, pairs), (virt_hbm, virt))
        )
    ]
    get_v.start()
    for copy in small:
        copy.start()
    get_a.start()
    get_prior.start()

    get_v.wait()
    meet_near()

    def block_at(px, pzl):
        return vb.at[y, pzl % 2, px, pzl // 2]

    for d in (2, 1, 3):
        start(
            block_at(x, zl), block_at(x, zl), z_send.at[d], z_recv.at[d], place(x, at(zl + d), y), s
        )
    for d in (2, 1, 3):
        landed(block_at(x, at(zl - d)), z_send.at[d], z_recv.at[d])

    for k in (0, 1):
        ref = vb.at[y, k, x]
        for d in (2, 1, 3):
            n = 4 * k + d
            start(ref, ref, x_send.at[n], x_recv.at[n], place(at(x + d), zl, y), s)
        for d in (1, 3, 2):
            n = 4 * k + d
            start(ref, ref, y_send.at[n], y_recv.at[n], place(x, zl, at(y + d)), s)

    for copy in small:
        copy.wait()
    slot_id = lax.broadcasted_iota(jnp.int32, (1, SLOTS), 1)
    block_id = lax.broadcasted_iota(jnp.int32, (64, SLOTS), 0)
    block_of = lax.broadcasted_iota(jnp.int32, (64, SLOTS), 1) >> 2
    held = jnp.broadcast_to(counts[...].astype(F32), (8, 64)).astype(BF16)
    before = dot_nn(held, jnp.where(block_id < block_of, 1.0, 0.0).astype(BF16))[0:1]
    own_count = dot_nn(held, jnp.where(block_id == block_of, 1.0, 0.0).astype(BF16))[0:1]
    within = (slot_id & 3).astype(F32)
    orbital_row = jnp.where(within < own_count, before + within, -1.0)
    match = lax.broadcasted_iota(jnp.int32, (NOCC, SLOTS), 0).astype(F32) == orbital_row
    pick = jnp.where(match, 1.0, 0.0).astype(BF16)
    get_a.wait()
    for i in range(CAPI):
        packed[i * NOCC:(i + 1) * NOCC, :] = dot_nn(
            pick, amps[i * SLOTS:(i + 1) * SLOTS, :]
        ).astype(BF16)

    def own_row(k):
        for d in (2, 1, 3):
            landed(vb.at[y, k, at(x - d)], x_send.at[4 * k + d], x_recv.at[4 * k + d])

    def opposite(k):
        ref = vb.at[y, k, at(x + 2)]
        for d in (1, 3, 2):
            n = 4 * k + d
            start(ref, ref, f_send.at[n], f_recv.at[n], place(x, zl, at(y + d)), s)

    def pass_on(k, d):
        n = 4 * k + d
        ref = vb.at[at(y - d), k, x]
        landed(ref, y_send.at[n], y_recv.at[n])
        start(ref, ref, s_send.at[2 * n], s_recv.at[2 * n], place(at(x + 1), zl, y), s)
        start(ref, ref, s_send.at[2 * n + 1], s_recv.at[2 * n + 1], place(at(x - 1), zl, y), s)

    def other_row(k, d):
        n = 4 * k + d
        row = at(y - d)
        landed(vb.at[row, k, at(x + 2)], f_send.at[n], f_recv.at[n])
        landed(vb.at[row, k, at(x - 1)], s_send.at[2 * n], s_recv.at[2 * n])
        landed(vb.at[row, k, at(x + 1)], s_send.at[2 * n + 1], s_recv.at[2 * n + 1])

    parts = ((0, 0), (0, 1), (1, 0), (-1, 0), (1, 1), (-1, 1), (2, 0), (2, 1))

    def multiply(*ts):
        blocks = []
        for t in ts:
            step, k = parts[t]
            blocks.append(vb[at(y + step), k].reshape(128, vb.shape[-1]))
        product = dot_nt(jnp.concatenate(blocks, axis=0), packed[...])
        for n, t in enumerate(ts):
            part[t] = product[128 * n:128 * (n + 1)].reshape(4, 2, 16, LIVE)
            start(part.at[t, :, other], core_in.at[t], c_send.at[t], c_recv.at[t], o, sibling)

    eye = lax.broadcasted_iota(jnp.int32, (16, GROUP), 0) == lax.broadcasted_iota(
        jnp.int32, (16, GROUP), 1
    )

    def code(values, out, top_out):
        top = jnp.maximum(jnp.max(jnp.abs(values), axis=1, keepdims=True), 1e-30)
        out[...] = jnp.round(values * (32767.0 / top)).astype(jnp.int32).astype(jnp.int16)
        top_out[...] = jnp.sum(jnp.where(eye, top, 0.0), axis=0, keepdims=True)

    def decode(coded, top_row):
        top = jnp.sum(jnp.where(eye, top_row, 0.0), axis=1, keepdims=True)
        return coded.astype(F32) * (top * (1.0 / 32767.0))

    def ahead(t):
        return (up, 1) if t % 2 else (down, -1)

    def behind(t):
        return ahead(t + 1)

    def send_coded(n, values, slab):
        code(values, r_out.at[n], top_out.at[n])
        start(r_out.at[n], r_in.at[n], r_send.at[n], r_recv.at[n], o, slab)
        start(top_out.at[n], top_in.at[n], m_send.at[n], m_recv.at[n], o, slab)

    def landed_coded(n):
        landed(r_in.at[n], r_send.at[n], r_recv.at[n])
        landed(top_in.at[n], m_send.at[n], m_recv.at[n])
        return decode(r_in[n], top_in[n])

    def add_cores(t):
        landed(core_in.at[t], c_send.at[t], c_recv.at[t])
        summed[t] = part[t, :, core] + core_in[t]
        send_coded(3 * t, summed[t, at(h + 2)], ahead(t)[0])
        slab, step = behind(t)
        send_coded(3 * t + 1, summed[t, at(h + step)], slab)

    def second(t):
        slab, step = ahead(t)
        values = summed[t, at(h + step)] + landed_coded(3 * t)
        send_coded(3 * t + 2, values, slab)

    def finish(t):
        step, k = parts[t]
        ladder[k, at(y + step)] = (
            summed[t, h] + landed_coded(3 * t + 1) + landed_coded(3 * t + 2)
        )

    pass_on(0, 1)
    pass_on(0, 3)
    own_row(0)
    multiply(0)
    opposite(0)
    pass_on(1, 1)
    pass_on(1, 3)
    own_row(1)
    multiply(1)
    opposite(1)
    pass_on(0, 2)
    meet_far()
    add_cores(0)
    pass_on(1, 2)
    add_cores(1)

    rest = jnp.broadcast_to(occ_energy[...], (8, NOCC))
    energy_row = jnp.zeros((8, SLOTS), F32)
    for _ in range(3):
        piece = rest.astype(BF16)
        rest = rest - piece.astype(F32)
        energy_row = energy_row + dot_nn(piece, pick)
    energy_row = energy_row[0:1]
    pair_total = pairs.shape[1]
    wanted = s * (GROUP // 2) + (lax.broadcasted_iota(jnp.int32, (GROUP, pair_total), 0) & 63)
    chosen = lax.broadcasted_iota(jnp.int32, (GROUP, pair_total), 1) == wanted
    label = lax.broadcasted_iota(jnp.int32, (GROUP, virt.shape[1]), 1).astype(F32)
    pair_energy = jnp.zeros((GROUP, 1), F32)
    for n in range(2):
        orbital = jnp.sum(
            jnp.where(chosen, pairs[n:n + 1, :].astype(F32), 0.0), axis=1, keepdims=True
        )
        pair_energy = pair_energy + jnp.sum(
            jnp.where(label == orbital, virt[...], 0.0), axis=1, keepdims=True
        )

    row_id = lax.broadcasted_iota(jnp.int32, (1024, SLOTS), 0)
    lane_id = lax.broadcasted_iota(jnp.int32, (1024, SLOTS), 1)
    wanted = (((row_id >> 6) & 3) << 6) + ((row_id >> 8) << 4) + ((row_id >> 2) & 15)
    orbital = jnp.sum(
        jnp.where(lane_id == wanted, orbital_row, 0.0), axis=1, keepdims=True
    ).astype(jnp.int32)
    slot_i = lax.broadcasted_iota(jnp.int32, (1024, 1), 0) & 3
    column = jnp.where(orbital >= 0, slot_i * NOCC + orbital, -1)
    onehot[...] = jnp.where(
        lax.broadcasted_iota(jnp.int32, (1024, LIVE), 1) == column, 1.0, 0.0
    ).astype(BF16)

    for t, k, d in ((2, 0, 3), (3, 0, 1), (4, 1, 3), (5, 1, 1), (6, 0, 2), (7, 1, 2)):
        other_row(k, d)
        multiply(t)
        if t >= 3:
            add_cores(t - 1)
    add_cores(7)
    for t in range(8):
        second(t)
    for t in range(8):
        finish(t)

    low = ladder[0].reshape(GROUP // 2, LIVE)
    top = ladder[1].reshape(GROUP // 2, LIVE)
    mirrored = jnp.concatenate([top, low], axis=0)
    peak = jnp.maximum(jnp.max(jnp.abs(mirrored), axis=1, keepdims=True), 1e-30)
    diagonal = lax.broadcasted_iota(jnp.int32, (GROUP, GROUP), 0) == lax.broadcasted_iota(
        jnp.int32, (GROUP, GROUP), 1
    )
    peaks[o] = jnp.sum(jnp.where(diagonal, peak, 0.0), axis=0, keepdims=True)

    def rows(b):
        return pl.ds(pl.multiple_of(b * 16, 16), 16)

    def exchange(dx, d, dy, sign=1):
        n = dx * 16 + d * 4 + dy
        px, pzl, py = at(x + sign * dx), at(zl + sign * d), at(y + sign * dy)
        b = place(px, pzl, py)
        source = o if sign > 0 else b
        return (
            remote(
                turned.at[rows(pzl * 16 + px * 4 + py)], arrived.at[rows(source)],
                e_send.at[n], e_recv.at[n], b, s,
            ),
            remote(peaks.at[source], peaks.at[source], p_send.at[n], p_recv.at[n], b, s),
        )

    whole = jnp.round(mirrored * (32767.0 / peak))
    coarse = jnp.round(whole * (1.0 / 256.0))
    fine = (whole - 256.0 * coarse).astype(BF16)
    coarse = coarse.astype(BF16)
    order = []
    for d in (2, 1, 3, 0):
        group = pl.ds(pl.multiple_of(at(zl + d) * 256, 256), 256)
        turned[group, :] = (
            256.0 * dot_nt(onehot[group, :], coarse) + dot_nt(onehot[group, :], fine)
        ).astype(jnp.int32).astype(jnp.int16)
        for dx in (2, 1, 3, 0):
            for dy in (2, 1, 3, 0):
                if dx or d or dy:
                    order.append((dx, d, dy))
                    for copy in exchange(dx, d, dy):
                        copy.start()
    arrived[rows(o), :] = turned[rows(zl * 16 + x * 4 + y), :]

    high, rest = halves(jnp.concatenate([low, top], axis=0))
    own = []
    for q in range(CAPI):
        cut = slice(q * NOCC, (q + 1) * NOCC)
        own.append(dot_nn(high[:, cut], pick) + dot_nn(rest[:, cut], pick))
    get_prior.wait()

    spread = jnp.where(
        lax.broadcasted_iota(jnp.int32, (SLOTS, SLOTS), 1)
        == ((lax.broadcasted_iota(jnp.int32, (SLOTS, SLOTS), 0) & 63) * 4
            + (lax.broadcasted_iota(jnp.int32, (SLOTS, SLOTS), 0) >> 6)),
        1.0, 0.0,
    ).astype(BF16)

    for copy in sends:
        copy.wait_send()

    for step in order:
        for copy in exchange(*step, sign=-1):
            copy.wait_recv()
        for copy in exchange(*step):
            copy.wait_send()

    opened[0:1024, :] = (
        arrived[...].astype(F32).reshape(64, 16, GROUP) * (peaks[...] * (1.0 / 32767.0))
    ).reshape(1024, GROUP)
    live = jnp.where(orbital_row >= 0.0, 1.0, 0.0)
    for q in range(CAPI):
        block = jnp.concatenate(
            [opened[pl.ds(q * CAPI + i, 64, stride=16), :] for i in range(CAPI)], axis=0
        )
        high, rest = halves(jnp.transpose(block))
        paired = own[q] + (dot_nn(high, spread) + dot_nn(rest, spread))
        mine = slot_id == o * CAPI + q
        energy = jnp.sum(jnp.where(mine, energy_row, 0.0), axis=1, keepdims=True)
        alive = jnp.sum(jnp.where(mine, live, 0.0), axis=1, keepdims=True)
        cut = slice(q * SLOTS, (q + 1) * SLOTS)
        fresh = prior[:, cut].astype(F32) + paired / ((energy + energy_row) - pair_energy)
        out_ref[:, cut] = jnp.where(alive * live > 0.5, fresh, 0.0)


def per_device(
    amplitudes, integrals, prior_amplitudes, occ_counts, occ_energy, pair_orbitals, virt_energy
):
    depth = amplitudes.shape[1]
    pair_count, virt_count = pair_orbitals.shape[1], virt_energy.shape[0]
    hbm_spec = pl.BlockSpec(memory_space=pltpu.HBM)
    vmem_spec = pl.BlockSpec(memory_space=pltpu.VMEM)
    dma = pltpu.SemaphoreType.DMA
    return pl.pallas_call(
        kernel,
        out_shape=pltpu.VMEM((GROUP, CAPI * SLOTS), F32),
        in_specs=[hbm_spec] * 7,
        out_specs=vmem_spec,
        scratch_shapes=[
            pltpu.VMEM((4, 2, 4, 2, 16, depth), BF16),
            pltpu.VMEM((CAPI * SLOTS, depth), BF16),
            pltpu.VMEM((GROUP, CAPI * SLOTS), BF16),
            pltpu.VMEM((1, occ_counts.shape[0]), jnp.int32),
            pltpu.VMEM((1, NOCC), F32),
            pltpu.VMEM((2, pair_count), jnp.int32),
            pltpu.VMEM((1, virt_count), F32),
            pltpu.VMEM((LIVE, depth), BF16),
            pltpu.VMEM((1024, LIVE), BF16),
            pltpu.VMEM((8, 4, 2, 16, LIVE), F32),
            pltpu.VMEM((8, 4, 16, LIVE), F32),
            pltpu.VMEM((8, 4, 16, LIVE), F32),
            pltpu.VMEM((2, 4, 16, LIVE), F32),
        ]
        + [pltpu.VMEM((24, 16, LIVE), jnp.int16)] * 2
        + [pltpu.VMEM((24, 1, GROUP), F32)] * 2
        + [pltpu.VMEM((1024, GROUP), jnp.int16)] * 2
        + [pltpu.VMEM((64, 1, GROUP), F32), pltpu.VMEM((1040, GROUP), F32)]
        + [pltpu.SemaphoreType.REGULAR] * 2
        + [
            dma((7,)), dma((4,)), dma((4,)), dma((8,)), dma((8,)), dma((8,)), dma((8,)), dma((8,)), dma((8,)),
            dma((16,)), dma((16,)),
            dma((8,)), dma((8,)), dma((24,)), dma((24,)), dma((24,)), dma((24,)), dma((64,)), dma((64,)),
            dma((64,)), dma((64,)),
        ],
        compiler_params=pltpu.CompilerParams(
            collective_id=0, has_side_effects=True, vmem_limit_bytes=58 * 1024 * 1024
        ),
        cost_estimate=pl.CostEstimate(flops=2 * 1024 * 640 * 768, bytes_accessed=3 << 20, transcendentals=0),
    )(
        integrals, amplitudes, prior_amplitudes,
        occ_counts[None, :], occ_energy[None, :], pair_orbitals, virt_energy[None, :],
    )


def solution(mesh):
    return jax.shard_map(
        per_device,
        mesh=mesh,
        in_specs=(P("occ", "slab"), P("occ", "slab"), P("slab", "occ"), P(), P(), P(), P()),
        out_specs=P("slab", "occ"),
        check_vma=False,
    )
```
